32 devices in a mesh: member: 2 (over y), lat: 8 (over z, core), lon: 2 (over x).
Axes of the slice: x: 2, y: 2, z: 4, core: 2. Of those that a mesh axis runs over, the one named last changes fastest.
Arguments:
- state: bfloat16 [72, 64, 256], P(None, 'lat', 'lon'), may hold values from -6 to 6
- noise: bfloat16 [2, 2, 8, 64, 256], P('member', None, None, 'lat', 'lon'), may hold values from -6 to 6
- target: bfloat16 [2, 72, 64, 256], P(None, None, 'lat', 'lon'), may hold values from -6 to 6
- encoder_state_weight: bfloat16 [512, 72], replicated, may hold values from -0.75 to 0.75
- enc_noise: bfloat16 [512, 8], replicated, may hold values from -2 to 2
- lat_taps: float32 [4, 7, 512], replicated, may hold values from -1.75 to 1.75
- lon_taps: float32 [4, 6, 512], replicated, may hold values from -1.75 to 1.75
- gains: float32 [4, 512], replicated, may hold values from 0.25 to 1.75
- mix: bfloat16 [4, 512, 512], replicated, may hold values from -0.25 to 0.25
- decode: bfloat16 [72, 512], replicated, may hold values from -0.25 to 0.25
Outputs:
- trajectory_predictions: bfloat16 [2, 2, 72, 64, 256], P('member', None, None, 'lat', 'lon')
- probabilistic_error: float32 [72, 64, 256], P('member', 'lat', 'lon')
The draws below stay inside these ranges and needn't reach their ends.
All inputs are finite; a program needn't handle non-finite values.
Results may differ from the reference program's by a relative error of at most 0.015.
Values may be sent and summed in bfloat16 or wider, within the bound.
A program may use at most 64 MiB of HBM per device.

```python
import jax
import jax.numpy as jnp
from jax import lax

C = 512
VAR = 72
NOISE = 8
LAYERS = 4
STEPS = 2
MEMBERS = 2
NLAT = 64
NLON = 256


def block_scale(own_key, shape, pieces, low, top_value):
    def one(position, blocks):
        steps = jax.random.uniform(jax.random.fold_in(jax.random.fold_in(own_key, 6), position), (blocks,), jnp.float32, low / len(pieces), top_value / len(pieces))
        return jnp.repeat(jnp.exp(steps), shape[position] // blocks).reshape((-1,) + (1,) * (len(shape) - position - 1))

    level = one(*pieces[0])
    for cut in pieces[1:]:
        level = level * one(*cut)
    return level


def gaussian(own_key, extent, scale, limit, shards=(), dtype=jnp.bfloat16):
    level = block_scale(own_key, extent, shards, -0.22, 0.18) if shards else 1.0
    entries = jax.random.normal(own_key, extent, jnp.float32) * scale * level
    return jnp.minimum(jnp.maximum(entries, -limit), limit).astype(dtype)


def setup_inputs(seed: int = 0) -> dict:
    streams_of = jax.random.split(jax.random.key(seed), 11)
    return {
        "state": gaussian(streams_of[0], (VAR, NLAT, NLON), 1.0, 6.0, ((1, 8), (2, 2))),
        "noise": gaussian(streams_of[1], (MEMBERS, STEPS, NOISE, NLAT, NLON), 1.0, 6.0, ((0, 2), (3, 8), (4, 2))),
        "target": gaussian(streams_of[2], (STEPS, VAR, NLAT, NLON), 1.0, 6.0, ((2, 8), (3, 2))),
        "encoder_state_weight": gaussian(streams_of[3], (C, VAR), VAR ** -0.5, 0.75),
        "enc_noise": gaussian(streams_of[4], (C, NOISE), NOISE ** -0.5, 2.0),
        "lat_taps": gaussian(streams_of[5], (LAYERS, 7, C), 13 ** -0.5, 1.75, (), jnp.float32),
        "lon_taps": gaussian(streams_of[6], (LAYERS, 6, C), 13 ** -0.5, 1.75, (), jnp.float32),
        "gains": jnp.clip(1.0 + 0.15 * jax.random.normal(streams_of[7], (LAYERS, C), jnp.float32), 0.25, 1.75),
        "mix": gaussian(streams_of[8], (LAYERS, C, C), C ** -0.5, 0.25),
        "decode": gaussian(streams_of[9], (VAR, C), C ** -0.5, 0.25),
    }


epsilon = 1e-05

def convolve(hidden, lat_row, lon_row):
    height = hidden.shape[1]
    width = hidden.shape[2]
    lat_pad = jnp.pad(hidden, ((0, 0), (3, 3), (0, 0)))
    lon_pad = jnp.concatenate([hidden[:, :, width - 3:], hidden, hidden[:, :, :3]], axis=2)
    total = jnp.zeros(hidden.shape, jnp.float32)
    for offset in range(7):
        total = total + lat_row[offset][:, None, None] * lat_pad[:, offset:offset + height, :].astype(jnp.float32)
    for column, offset in enumerate([0, 1, 2, 4, 5, 6]):
        total = total + lon_row[column][:, None, None] * lon_pad[:, :, offset:offset + width].astype(jnp.float32)
    return total

def layer_step(hidden, lat_row, lon_row, gain_row, matrix):
    conv = convolve(hidden, lat_row, lon_row)
    center = lax.optimization_barrier(jnp.mean(conv, axis=0))
    variance = lax.optimization_barrier(jnp.mean(jnp.square(conv - center), axis=0))
    normalized_fields = ((conv - center) * lax.rsqrt(variance + epsilon) * gain_row[:, None, None]).astype(jnp.bfloat16)
    channel_list = hidden.shape[0]
    mixed = jnp.dot(matrix, normalized_fields.reshape(channel_list, -1), preferred_element_type=jnp.float32).reshape(hidden.shape)
    return (hidden.astype(jnp.float32) + jax.nn.gelu(mixed, approximate=True)).astype(jnp.bfloat16)

def reference(state, noise, target, encoder_state_weight, enc_noise, lat_taps, lon_taps, gains, mix, decode):
    members = noise.shape[0]
    step_count = noise.shape[1]
    layer_count = mix.shape[0]
    channel_list = mix.shape[1]
    quantity_total, height, width = state.shape
    noise_count = noise.shape[2]
    whole_ensemble_grids = []
    for member_id in range(members):
        current = state
        increment_errors = []
        for step in range(step_count):
            hidden = jnp.dot(encoder_state_weight, current.reshape(quantity_total, -1), preferred_element_type=jnp.float32) + jnp.dot(enc_noise, noise[member_id, step].reshape(noise_count, -1), preferred_element_type=jnp.float32)
            hidden = hidden.reshape(channel_list, height, width).astype(jnp.bfloat16)
            for level in range(layer_count):
                hidden = layer_step(hidden, lat_taps[level], lon_taps[level], gains[level], mix[level])
            decoded = jnp.dot(decode, hidden.reshape(channel_list, -1), preferred_element_type=jnp.float32).reshape(quantity_total, height, width)
            current = (current.astype(jnp.float32) + decoded).astype(jnp.bfloat16)
            increment_errors.append(current)
        whole_ensemble_grids.append(jnp.stack(increment_errors))
    trajectory_predictions = jnp.stack(whole_ensemble_grids)
    quantities_real = trajectory_predictions.astype(jnp.float32)
    skill = lax.optimization_barrier(jnp.sum(jnp.abs(quantities_real - target.astype(jnp.float32)[None]), axis=(0, 1)))
    spread = jnp.zeros((quantity_total, height, width), jnp.float32)
    for other in range(members):
        spread = spread + lax.optimization_barrier(jnp.sum(jnp.abs(quantities_real - quantities_real[other][None]), axis=(0, 1)))
    scale = float(members)
    probabilistic_error = skill / scale - spread / (2.0 * scale * (scale - 1.0))
    return (trajectory_predictions, probabilistic_error)
```

```python
import functools

import jax
import jax.numpy as jnp
import numpy as np
from jax import lax
from jax.experimental import pallas as pl
from jax.experimental.pallas import tpu as pltpu
from jax.sharding import PartitionSpec as P

MESH = pl.DeviceIdType.MESH
epsilon = 1e-05
REACH = 3
CHUNK = 16


def edge_maps(rows, cols):
    edges = 2 * REACH
    fold = 2
    lanes = cols // fold
    assert rows * edges <= lanes
    take = np.zeros((fold, rows * cols, cols), np.float32)
    for half in range(fold):
        for row in range(rows):
            for k in range(edges):
                col = k if k < REACH else cols - edges + k
                take[half, row * cols + col, half * lanes + row * edges + k] = 1.0
    return take, take.transpose(0, 2, 1)


def rollout_kernel(
    count,
    layers,
    state,
    noise,
    taps,
    enc_state,
    enc_noise,
    mix,
    decode,
    take,
    give,
    trajectory,
    field,
    conv,
    edge,
    current,
    normed,
    sums,
    packed_out,
    packed_in,
    send_sem,
    recv_sem,
):
    rows, _, cols = state.shape
    channels = mix.shape[1]
    half = channels // 2
    steps = noise.shape[0]
    total_layers = steps * layers
    me = lax.axis_index("lat")
    peer = 1 - lax.axis_index("lon")
    has_up = me > 0
    has_down = me < count - 1

    zero = jnp.zeros((REACH, channels, cols), jnp.bfloat16)
    for slot in range(2):
        field[slot, 0:REACH] = zero
        field[slot, REACH + rows : 2 * REACH + rows] = zero
    current[...] = state[...]

    barrier = pltpu.get_barrier_semaphore()

    @pl.when(has_up)
    def _():
        pl.semaphore_signal(barrier, inc=1, device_id={"lat": me - 1}, device_id_type=MESH)

    @pl.when(has_down)
    def _():
        pl.semaphore_signal(barrier, inc=1, device_id={"lat": me + 1}, device_id_type=MESH)

    pl.semaphore_signal(barrier, inc=1, device_id={"lon": peer}, device_id_type=MESH)
    pl.semaphore_wait(barrier, 1 + has_up.astype(jnp.int32) + has_down.astype(jnp.int32))

    def copy_up(slot):
        return pltpu.make_async_remote_copy(
            src_ref=field.at[slot, pl.ds(REACH, REACH)],
            dst_ref=field.at[slot, pl.ds(REACH + rows, REACH)],
            send_sem=send_sem.at[slot, 0],
            recv_sem=recv_sem.at[slot, 0],
            device_id={"lat": me - 1},
            device_id_type=MESH,
        )

    def copy_down(slot):
        return pltpu.make_async_remote_copy(
            src_ref=field.at[slot, pl.ds(rows, REACH)],
            dst_ref=field.at[slot, pl.ds(0, REACH)],
            send_sem=send_sem.at[slot, 1],
            recv_sem=recv_sem.at[slot, 1],
            device_id={"lat": me + 1},
            device_id_type=MESH,
        )

    def copy_across(slot):
        return pltpu.make_async_remote_copy(
            src_ref=packed_out.at[slot],
            dst_ref=packed_in.at[slot],
            send_sem=send_sem.at[slot, 2],
            recv_sem=recv_sem.at[slot, 2],
            device_id={"lon": peer},
            device_id_type=MESH,
        )

    def start_lat(slot):
        @pl.when(has_up)
        def _():
            copy_up(slot).start()

        @pl.when(has_down)
        def _():
            copy_down(slot).start()

    def start_lon(slot):
        total = None
        for part in range(2):
            strip = jnp.concatenate(
                [field[slot, REACH + row, part * half : (part + 1) * half] for row in range(rows)],
                axis=1,
            )
            term = jnp.dot(strip, take[part], preferred_element_type=jnp.float32)
            total = term if total is None else total + term
        packed_out[slot] = total.astype(jnp.bfloat16)
        copy_across(slot).start()

    def finish(slot):
        @pl.when(has_up)
        def _():
            copy_up(slot).wait_send()
            copy_down(slot).wait_recv()

        @pl.when(has_down)
        def _():
            copy_down(slot).wait_send()
            copy_up(slot).wait_recv()

        copy_across(slot).wait()
        for part in range(2):
            wide = jnp.dot(
                packed_in[slot], give[part], preferred_element_type=jnp.float32
            ).astype(jnp.bfloat16)
            for row in range(rows):
                edge[row, part * half : (part + 1) * half] = wide[:, row * cols : (row + 1) * cols]

    def encode(step, slot):
        for row in range(rows):
            hidden = jnp.dot(
                enc_state[...], current[row], preferred_element_type=jnp.float32
            ) + jnp.dot(enc_noise[...], noise[step, row], preferred_element_type=jnp.float32)
            field[slot, REACH + row] = hidden.astype(jnp.bfloat16)

    def tap(layer, at, index):
        return jnp.broadcast_to(taps[layer, pl.ds(at, CHUNK), index : index + 1], (CHUNK, cols))

    def own_rows(layer, slot):
        @pl.loop(0, channels // CHUNK)
        def _(block):
            at = pl.multiple_of(block * CHUNK, CHUNK)
            weights = [tap(layer, at, d) for d in range(2 * REACH + 1)]
            totals = [None] * rows
            for source in range(rows):
                x = field[slot, REACH + source, pl.ds(at, CHUNK)].astype(jnp.float32)
                for row in range(max(0, source - REACH), min(rows, source + REACH + 1)):
                    term = weights[source - row + REACH] * x
                    totals[row] = term if totals[row] is None else totals[row] + term
            for row in range(rows):
                conv[row, pl.ds(at, CHUNK)] = totals[row]

    def edge_rows(layer, slot):
        sums[...] = jnp.zeros(sums.shape, jnp.float32)
        lane = lax.broadcasted_iota(jnp.int32, (CHUNK, cols), 1)

        @pl.loop(0, channels // CHUNK)
        def _(block):
            at = pl.multiple_of(block * CHUNK, CHUNK)
            weights = [tap(layer, at, d) for d in range(4 * REACH + 1)]
            for row in range(rows):
                total = conv[row, pl.ds(at, CHUNK)]
                for source in range(row - REACH, row + REACH + 1):
                    if source < 0 or source >= rows:
                        x = field[slot, REACH + source, pl.ds(at, CHUNK)].astype(jnp.float32)
                        total = total + weights[source - row + REACH] * x
                x = field[slot, REACH + row, pl.ds(at, CHUNK)].astype(jnp.float32)
                far = edge[row, pl.ds(at, CHUNK)].astype(jnp.float32)
                index = 2 * REACH + 1
                for d in range(-REACH, REACH + 1):
                    if d == 0:
                        continue
                    outside = lane >= cols + d if d < 0 else lane < d
                    moved = pltpu.roll(jnp.where(outside, far, x), (-d) % cols, 1)
                    total = total + weights[index] * moved
                    index += 1
                conv[row, pl.ds(at, CHUNK)] = total
                square = total * total
                sums[0, row] += total[0:8] + total[8:16]
                sums[1, row] += square[0:8] + square[8:16]

    def mix_pair(layer, slot, following, pair):
        for place, row in enumerate(pair):
            center = jnp.sum(sums[0, row], axis=0, keepdims=True) / channels
            second = jnp.sum(sums[1, row], axis=0, keepdims=True) / channels
            scale = lax.rsqrt(jnp.maximum(second - center * center, 0.0) + epsilon)
            gain = taps[layer, :, 4 * REACH + 1 : 4 * REACH + 2]
            normed[:, place * cols : (place + 1) * cols] = (
                (conv[row] - center) * scale * gain
            ).astype(jnp.bfloat16)

        @pl.loop(0, channels // 128)
        def _(block):
            at = pl.multiple_of(block * 128, 128)
            mixed = jnp.dot(
                mix[layer, pl.ds(at, 128)], normed[...], preferred_element_type=jnp.float32
            )
            bent = mixed * (0.7978845608028654 + 0.035677408136300125 * (mixed * mixed))
            half_mixed = 0.5 * mixed
            bump = half_mixed + half_mixed * jnp.tanh(bent)
            for place, row in enumerate(pair):
                held = field[slot, REACH + row, pl.ds(at, 128)].astype(jnp.float32)
                field[following, REACH + row, pl.ds(at, 128)] = (
                    held + bump[:, place * cols : (place + 1) * cols]
                ).astype(jnp.bfloat16)

    encode(0, 0)
    start_lat(0)
    start_lon(0)

    outer = list(range(REACH)) + list(range(rows - 1, rows - 1 - REACH, -1))
    inner = list(range(REACH, rows - REACH))

    def pairs(items):
        return [items[k : k + 2] for k in range(0, len(items), 2)]

    @pl.loop(0, total_layers)
    def _(index):
        slot = index % 2
        following = 1 - slot
        layer = index % layers
        step = index // layers
        last = layer == layers - 1
        own_rows(layer, slot)
        finish(slot)
        edge_rows(layer, slot)
        for pair in pairs(outer):
            mix_pair(layer, slot, following, pair)

        @pl.when(jnp.logical_not(last))
        def _():
            start_lat(following)

        for pair in pairs(inner):
            mix_pair(layer, slot, following, pair)

        @pl.when(last)
        def _():
            for row in range(rows):
                decoded = jnp.dot(
                    decode[...], field[following, REACH + row], preferred_element_type=jnp.float32
                )
                fresh = (current[row].astype(jnp.float32) + decoded).astype(jnp.bfloat16)
                current[row] = fresh
                trajectory[step, row] = fresh

            @pl.when(step < steps - 1)
            def _():
                encode(step + 1, following)
                start_lat(following)

        @pl.when(index < total_layers - 1)
        def _():
            start_lon(following)


def rollout(count, state, noise, encoder_state_weight, enc_noise, lat_taps, lon_taps, gains, mix, decode):
    quantities, rows, cols = state.shape
    steps = noise.shape[1]
    layers, channels, _ = mix.shape
    take, give = edge_maps(rows, cols)
    table = jnp.concatenate([lat_taps, lon_taps, gains[:, None]], axis=1).transpose(0, 2, 1)
    vmem = pl.BlockSpec(memory_space=pltpu.VMEM)
    return pl.pallas_call(
        functools.partial(rollout_kernel, count, layers),
        out_shape=jax.ShapeDtypeStruct((steps, rows, quantities, cols), jnp.bfloat16),
        in_specs=[vmem] * 9,
        out_specs=vmem,
        scratch_shapes=[
            pltpu.VMEM((2, rows + 2 * REACH, channels, cols), jnp.bfloat16),
            pltpu.VMEM((rows, channels, cols), jnp.float32),
            pltpu.VMEM((rows, channels, cols), jnp.bfloat16),
            pltpu.VMEM((rows, quantities, cols), jnp.bfloat16),
            pltpu.VMEM((channels, 2 * cols), jnp.bfloat16),
            pltpu.VMEM((2, rows, 8, cols), jnp.float32),
            pltpu.VMEM((2, channels // 2, cols), jnp.bfloat16),
            pltpu.VMEM((2, channels // 2, cols), jnp.bfloat16),
            pltpu.SemaphoreType.DMA((2, 3)),
            pltpu.SemaphoreType.DMA((2, 3)),
        ],
        compiler_params=pltpu.CompilerParams(
            collective_id=0, has_side_effects=True, vmem_limit_bytes=40 * 1024 * 1024
        ),
    )(
        state.transpose(1, 0, 2),
        noise[0].transpose(0, 2, 1, 3),
        table,
        encoder_state_weight,
        enc_noise,
        mix,
        decode,
        jnp.asarray(take, jnp.bfloat16),
        jnp.asarray(give, jnp.bfloat16),
    )


def local(
    count, state, noise, target, encoder_state_weight, enc_noise, lat_taps, lon_taps, gains, mix, decode
):
    quantity_total = state.shape[0]
    forecast = rollout(
        count, state, noise, encoder_state_weight, enc_noise, lat_taps, lon_taps, gains, mix, decode
    )
    trajectory_predictions = forecast.transpose(0, 2, 1, 3)[None]
    members = lax.axis_size("member")
    scale = float(members)
    regrouped = lax.all_to_all(
        trajectory_predictions, "member", split_axis=2, concat_axis=0, tiled=True
    )
    quantities_real = regrouped.astype(jnp.float32)
    block = quantity_total // members
    start = lax.axis_index("member") * block
    target_block = lax.dynamic_slice_in_dim(target, start, block, 1).astype(jnp.float32)
    skill = jnp.sum(jnp.abs(quantities_real - target_block[None]), axis=(0, 1))
    spread = jnp.zeros(skill.shape, jnp.float32)
    for other in range(members):
        spread = spread + jnp.sum(jnp.abs(quantities_real - quantities_real[other][None]), axis=(0, 1))
    probabilistic_error = skill / scale - spread / (2.0 * scale * (scale - 1.0))
    return (trajectory_predictions, probabilistic_error)


def solution(mesh):
    assert mesh.shape["lon"] == 2
    in_specs = (
        P(None, "lat", "lon"),
        P("member", None, None, "lat", "lon"),
        P(None, None, "lat", "lon"),
        P(),
        P(),
        P(),
        P(),
        P(),
        P(),
        P(),
    )
    out_specs = (P("member", None, None, "lat", "lon"), P("member", "lat", "lon"))
    return jax.shard_map(
        functools.partial(local, mesh.shape["lat"]),
        mesh=mesh,
        in_specs=in_specs,
        out_specs=out_specs,
        check_vma=False,
    )
```

```python
import functools

import jax
import jax.numpy as jnp
import numpy as np
from jax import lax
from jax.experimental import pallas as pl
from jax.experimental.pallas import tpu as pltpu
from jax.sharding import PartitionSpec as P

MESH = pl.DeviceIdType.MESH
epsilon = 1e-05
REACH = 3
CHUNK = 16


def edge_maps(rows, cols):
    edges = 2 * REACH
    fold = 2
    lanes = cols // fold
    assert rows * edges <= lanes
    take = np.zeros((fold, rows * cols, cols), np.float32)
    for half in range(fold):
        for row in range(rows):
            for k in range(edges):
                col = k if k < REACH else cols - edges + k
                take[half, row * cols + col, half * lanes + row * edges + k] = 1.0
    return take, take.transpose(0, 2, 1)


def rollout_kernel(
    count,
    layers,
    state,
    noise,
    taps,
    enc_state,
    enc_noise,
    mix,
    decode,
    take,
    give,
    trajectory,
    field,
    conv,
    edge,
    current,
    normed,
    sums,
    packed_out,
    packed_in,
    send_sem,
    recv_sem,
):
    rows, _, cols = state.shape
    channels = mix.shape[1]
    half = channels // 2
    steps = noise.shape[0]
    total_layers = steps * layers
    me = lax.axis_index("lat")
    peer = 1 - lax.axis_index("lon")
    has_up = me > 0
    has_down = me < count - 1

    zero = jnp.zeros((REACH, channels, cols), jnp.bfloat16)
    for slot in range(2):
        field[slot, 0:REACH] = zero
        field[slot, REACH + rows : 2 * REACH + rows] = zero
    current[...] = state[...]

    barrier = pltpu.get_barrier_semaphore()

    @pl.when(has_up)
    def _():
        pl.semaphore_signal(barrier, inc=1, device_id={"lat": me - 1}, device_id_type=MESH)

    @pl.when(has_down)
    def _():
        pl.semaphore_signal(barrier, inc=1, device_id={"lat": me + 1}, device_id_type=MESH)

    pl.semaphore_signal(barrier, inc=1, device_id={"lon": peer}, device_id_type=MESH)
    pl.semaphore_wait(barrier, 1 + has_up.astype(jnp.int32) + has_down.astype(jnp.int32))

    def copy_up(slot):
        return pltpu.make_async_remote_copy(
            src_ref=field.at[slot, pl.ds(REACH, REACH)],
            dst_ref=field.at[slot, pl.ds(REACH + rows, REACH)],
            send_sem=send_sem.at[slot, 0],
            recv_sem=recv_sem.at[slot, 0],
            device_id={"lat": me - 1},
            device_id_type=MESH,
        )

    def copy_down(slot):
        return pltpu.make_async_remote_copy(
            src_ref=field.at[slot, pl.ds(rows, REACH)],
            dst_ref=field.at[slot, pl.ds(0, REACH)],
            send_sem=send_sem.at[slot, 1],
            recv_sem=recv_sem.at[slot, 1],
            device_id={"lat": me + 1},
            device_id_type=MESH,
        )

    def copy_across(slot):
        return pltpu.make_async_remote_copy(
            src_ref=packed_out.at[slot],
            dst_ref=packed_in.at[slot],
            send_sem=send_sem.at[slot, 2],
            recv_sem=recv_sem.at[slot, 2],
            device_id={"lon": peer},
            device_id_type=MESH,
        )

    def start_lat(slot):
        @pl.when(has_up)
        def _():
            copy_up(slot).start()

        @pl.when(has_down)
        def _():
            copy_down(slot).start()

    def start_lon(slot):
        total = None
        for part in range(2):
            strip = jnp.concatenate(
                [field[slot, REACH + row, part * half : (part + 1) * half] for row in range(rows)],
                axis=1,
            )
            term = jnp.dot(strip, take[part], preferred_element_type=jnp.float32)
            total = term if total is None else total + term
        packed_out[slot] = total.astype(jnp.bfloat16)
        copy_across(slot).start()

    def finish(slot):
        @pl.when(has_up)
        def _():
            copy_up(slot).wait_send()
            copy_down(slot).wait_recv()

        @pl.when(has_down)
        def _():
            copy_down(slot).wait_send()
            copy_up(slot).wait_recv()

        copy_across(slot).wait()
        for part in range(2):
            wide = jnp.dot(
                packed_in[slot], give[part], preferred_element_type=jnp.float32
            ).astype(jnp.bfloat16)
            for row in range(rows):
                edge[row, part * half : (part + 1) * half] = wide[:, row * cols : (row + 1) * cols]

    def encode(step, slot):
        for row in range(rows):
            hidden = jnp.dot(
                enc_state[...], current[row], preferred_element_type=jnp.float32
            ) + jnp.dot(enc_noise[...], noise[step, row], preferred_element_type=jnp.float32)
            field[slot, REACH + row] = hidden.astype(jnp.bfloat16)

    def tap(layer, at, index):
        return jnp.broadcast_to(taps[layer, pl.ds(at, CHUNK), index : index + 1], (CHUNK, cols))

    def own_rows(layer, slot):
        @pl.loop(0, channels // CHUNK)
        def _(block):
            at = pl.multiple_of(block * CHUNK, CHUNK)
            weights = [tap(layer, at, d) for d in range(2 * REACH + 1)]
            totals = [None] * rows
            for source in range(rows):
                x = field[slot, REACH + source, pl.ds(at, CHUNK)].astype(jnp.float32)
                for row in range(max(0, source - REACH), min(rows, source + REACH + 1)):
                    term = weights[source - row + REACH] * x
                    totals[row] = term if totals[row] is None else totals[row] + term
            for row in range(rows):
                conv[row, pl.ds(at, CHUNK)] = totals[row]

    def edge_rows(layer, slot):
        sums[...] = jnp.zeros(sums.shape, jnp.float32)
        lane = lax.broadcasted_iota(jnp.int32, (CHUNK, cols), 1)

        @pl.loop(0, channels // CHUNK)
        def _(block):
            at = pl.multiple_of(block * CHUNK, CHUNK)
            weights = [tap(layer, at, d) for d in range(4 * REACH + 1)]
            near = [field[slot, k, pl.ds(at, CHUNK)] for k in range(rows + 2 * REACH)]
            far = [edge[row, pl.ds(at, CHUNK)] for row in range(rows)]
            totals = [conv[row, pl.ds(at, CHUNK)] for row in range(rows)]
            for row in range(rows):
                for source in range(row - REACH, row + REACH + 1):
                    if source < 0 or source >= rows:
                        x = near[REACH + source].astype(jnp.float32)
                        totals[row] = totals[row] + weights[source - row + REACH] * x
            index = 2 * REACH + 1
            for d in range(-REACH, REACH + 1):
                if d == 0:
                    continue
                outside = lane >= cols + d if d < 0 else lane < d
                for row in range(rows):
                    source = jnp.where(outside, far[row], near[REACH + row])
                    totals[row] = totals[row] + weights[index] * pltpu.roll(source, (-d) % cols, 1).astype(jnp.float32)
                index += 1
            for row in range(rows):
                square = totals[row] * totals[row]
                conv[row, pl.ds(at, CHUNK)] = totals[row]
                sums[0, row] += totals[row][0:8] + totals[row][8:16]
                sums[1, row] += square[0:8] + square[8:16]

    def mix_pair(layer, slot, following, pair):
        for place, row in enumerate(pair):
            center = jnp.sum(sums[0, row], axis=0, keepdims=True) / channels
            second = jnp.sum(sums[1, row], axis=0, keepdims=True) / channels
            scale = lax.rsqrt(jnp.maximum(second - center * center, 0.0) + epsilon)
            gain = taps[layer, :, 4 * REACH + 1 : 4 * REACH + 2]
            normed[:, place * cols : (place + 1) * cols] = (
                (conv[row] - center) * scale * gain
            ).astype(jnp.bfloat16)

        mixed = jnp.dot(mix[layer], normed[...], preferred_element_type=jnp.float32)
        bent = mixed * (0.7978845608028654 + 0.035677408136300125 * (mixed * mixed))
        half_mixed = 0.5 * mixed
        bump = half_mixed + half_mixed * jnp.tanh(bent)
        held = [field[slot, REACH + row].astype(jnp.float32) for row in pair]
        for place, row in enumerate(pair):
            field[following, REACH + row] = (
                held[place] + bump[:, place * cols : (place + 1) * cols]
            ).astype(jnp.bfloat16)

    encode(0, 0)
    start_lat(0)
    start_lon(0)

    outer = list(range(REACH)) + list(range(rows - 1, rows - 1 - REACH, -1))
    inner = list(range(REACH, rows - REACH))

    def pairs(items):
        return [items[k : k + 2] for k in range(0, len(items), 2)]

    @pl.loop(0, total_layers)
    def _(index):
        slot = index % 2
        following = 1 - slot
        layer = index % layers
        step = index // layers
        last = layer == layers - 1
        own_rows(layer, slot)
        finish(slot)
        edge_rows(layer, slot)
        for pair in pairs(outer):
            mix_pair(layer, slot, following, pair)

        @pl.when(jnp.logical_not(last))
        def _():
            start_lat(following)

        for pair in pairs(inner):
            mix_pair(layer, slot, following, pair)

        @pl.when(last)
        def _():
            for row in range(rows):
                decoded = jnp.dot(
                    decode[...], field[following, REACH + row], preferred_element_type=jnp.float32
                )
                fresh = (current[row].astype(jnp.float32) + decoded).astype(jnp.bfloat16)
                current[row] = fresh
                trajectory[step, row] = fresh

            @pl.when(step < steps - 1)
            def _():
                encode(step + 1, following)
                start_lat(following)

        @pl.when(index < total_layers - 1)
        def _():
            start_lon(following)


def rollout(count, state, noise, encoder_state_weight, enc_noise, lat_taps, lon_taps, gains, mix, decode):
    quantities, rows, cols = state.shape
    steps = noise.shape[1]
    layers, channels, _ = mix.shape
    take, give = edge_maps(rows, cols)
    table = jnp.concatenate([lat_taps, lon_taps, gains[:, None]], axis=1).transpose(0, 2, 1)
    vmem = pl.BlockSpec(memory_space=pltpu.VMEM)
    return pl.pallas_call(
        functools.partial(rollout_kernel, count, layers),
        out_shape=jax.ShapeDtypeStruct((steps, rows, quantities, cols), jnp.bfloat16),
        in_specs=[vmem] * 9,
        out_specs=vmem,
        scratch_shapes=[
            pltpu.VMEM((2, rows + 2 * REACH, channels, cols), jnp.bfloat16),
            pltpu.VMEM((rows, channels, cols), jnp.float32),
            pltpu.VMEM((rows, channels, cols), jnp.bfloat16),
            pltpu.VMEM((rows, quantities, cols), jnp.bfloat16),
            pltpu.VMEM((channels, 2 * cols), jnp.bfloat16),
            pltpu.VMEM((2, rows, 8, cols), jnp.float32),
            pltpu.VMEM((2, channels // 2, cols), jnp.bfloat16),
            pltpu.VMEM((2, channels // 2, cols), jnp.bfloat16),
            pltpu.SemaphoreType.DMA((2, 3)),
            pltpu.SemaphoreType.DMA((2, 3)),
        ],
        compiler_params=pltpu.CompilerParams(
            collective_id=0, has_side_effects=True, vmem_limit_bytes=40 * 1024 * 1024
        ),
    )(
        state.transpose(1, 0, 2),
        noise[0].transpose(0, 2, 1, 3),
        table,
        encoder_state_weight,
        enc_noise,
        mix,
        decode,
        jnp.asarray(take, jnp.bfloat16),
        jnp.asarray(give, jnp.bfloat16),
    )


def local(
    count, state, noise, target, encoder_state_weight, enc_noise, lat_taps, lon_taps, gains, mix, decode
):
    quantity_total = state.shape[0]
    forecast = rollout(
        count, state, noise, encoder_state_weight, enc_noise, lat_taps, lon_taps, gains, mix, decode
    )
    trajectory_predictions = forecast.transpose(0, 2, 1, 3)[None]
    members = lax.axis_size("member")
    scale = float(members)
    regrouped = lax.all_to_all(
        trajectory_predictions, "member", split_axis=2, concat_axis=0, tiled=True
    )
    quantities_real = regrouped.astype(jnp.float32)
    block = quantity_total // members
    start = lax.axis_index("member") * block
    target_block = lax.dynamic_slice_in_dim(target, start, block, 1).astype(jnp.float32)
    skill = jnp.sum(jnp.abs(quantities_real - target_block[None]), axis=(0, 1))
    spread = jnp.zeros(skill.shape, jnp.float32)
    for other in range(members):
        spread = spread + jnp.sum(jnp.abs(quantities_real - quantities_real[other][None]), axis=(0, 1))
    probabilistic_error = skill / scale - spread / (2.0 * scale * (scale - 1.0))
    return (trajectory_predictions, probabilistic_error)


def solution(mesh):
    assert mesh.shape["lon"] == 2
    in_specs = (
        P(None, "lat", "lon"),
        P("member", None, None, "lat", "lon"),
        P(None, None, "lat", "lon"),
        P(),
        P(),
        P(),
        P(),
        P(),
        P(),
        P(),
    )
    out_specs = (P("member", None, None, "lat", "lon"), P("member", "lat", "lon"))
    return jax.shard_map(
        functools.partial(local, mesh.shape["lat"]),
        mesh=mesh,
        in_specs=in_specs,
        out_specs=out_specs,
        check_vma=False,
    )
```

```python
import functools

import jax
import jax.numpy as jnp
import numpy as np
from jax import lax
from jax.experimental import pallas as pl
from jax.experimental.pallas import tpu as pltpu
from jax.sharding import PartitionSpec as P

MESH = pl.DeviceIdType.MESH
epsilon = 1e-05
REACH = 3
CHUNK = 16


def edge_maps(rows, cols):
    edges = 2 * REACH
    fold = 2
    lanes = cols // fold
    assert rows * edges <= lanes
    take = np.zeros((fold, rows * cols, cols), np.float32)
    for half in range(fold):
        for row in range(rows):
            for k in range(edges):
                col = k if k < REACH else cols - edges + k
                take[half, row * cols + col, half * lanes + row * edges + k] = 1.0
    return take, take.transpose(0, 2, 1)


def rollout_kernel(
    count,
    layers,
    state,
    noise,
    taps,
    enc_state,
    enc_noise,
    mix,
    decode,
    take,
    give,
    trajectory,
    field,
    conv,
    edge,
    current,
    normed,
    sums,
    packed_out,
    packed_in,
    send_sem,
    recv_sem,
):
    rows, _, cols = state.shape
    channels = mix.shape[1]
    half = channels // 2
    steps = noise.shape[0]
    total_layers = steps * layers
    me = lax.axis_index("lat")
    peer = 1 - lax.axis_index("lon")
    has_up = me > 0
    has_down = me < count - 1

    zero = jnp.zeros((REACH, channels, cols), jnp.bfloat16)
    for slot in range(2):
        field[slot, 0:REACH] = zero
        field[slot, REACH + rows : 2 * REACH + rows] = zero
    current[...] = state[...]

    barrier = pltpu.get_barrier_semaphore()

    @pl.when(has_up)
    def _():
        pl.semaphore_signal(barrier, inc=1, device_id={"lat": me - 1}, device_id_type=MESH)

    @pl.when(has_down)
    def _():
        pl.semaphore_signal(barrier, inc=1, device_id={"lat": me + 1}, device_id_type=MESH)

    pl.semaphore_signal(barrier, inc=1, device_id={"lon": peer}, device_id_type=MESH)
    pl.semaphore_wait(barrier, 1 + has_up.astype(jnp.int32) + has_down.astype(jnp.int32))

    def copy_up(slot):
        return pltpu.make_async_remote_copy(
            src_ref=field.at[slot, pl.ds(REACH, REACH)],
            dst_ref=field.at[slot, pl.ds(REACH + rows, REACH)],
            send_sem=send_sem.at[slot, 0],
            recv_sem=recv_sem.at[slot, 0],
            device_id={"lat": me - 1},
            device_id_type=MESH,
        )

    def copy_down(slot):
        return pltpu.make_async_remote_copy(
            src_ref=field.at[slot, pl.ds(rows, REACH)],
            dst_ref=field.at[slot, pl.ds(0, REACH)],
            send_sem=send_sem.at[slot, 1],
            recv_sem=recv_sem.at[slot, 1],
            device_id={"lat": me + 1},
            device_id_type=MESH,
        )

    def copy_across(slot):
        return pltpu.make_async_remote_copy(
            src_ref=packed_out.at[slot],
            dst_ref=packed_in.at[slot],
            send_sem=send_sem.at[slot, 2],
            recv_sem=recv_sem.at[slot, 2],
            device_id={"lon": peer},
            device_id_type=MESH,
        )

    def start_lat(slot):
        @pl.when(has_up)
        def _():
            copy_up(slot).start()

        @pl.when(has_down)
        def _():
            copy_down(slot).start()

    def start_lon(slot):
        total = None
        for part in range(2):
            strip = jnp.concatenate(
                [field[slot, REACH + row, part * half : (part + 1) * half] for row in range(rows)],
                axis=1,
            )
            term = jnp.dot(strip, take[part], preferred_element_type=jnp.float32)
            total = term if total is None else total + term
        packed_out[slot] = total.astype(jnp.bfloat16)
        copy_across(slot).start()

    def finish(slot):
        @pl.when(has_up)
        def _():
            copy_up(slot).wait_send()
            copy_down(slot).wait_recv()

        @pl.when(has_down)
        def _():
            copy_down(slot).wait_send()
            copy_up(slot).wait_recv()

        copy_across(slot).wait()
        for part in range(2):
            wide = jnp.dot(
                packed_in[slot], give[part], preferred_element_type=jnp.float32
            ).astype(jnp.bfloat16)
            for row in range(rows):
                edge[row, part * half : (part + 1) * half] = wide[:, row * cols : (row + 1) * cols]

    def encode(step, slot):
        for row in range(rows):
            hidden = jnp.dot(
                enc_state[...], current[row], preferred_element_type=jnp.float32
            ) + jnp.dot(enc_noise[...], noise[step, row], preferred_element_type=jnp.float32)
            field[slot, REACH + row] = hidden.astype(jnp.bfloat16)

    def tap(layer, at, index):
        column = taps[layer, pl.ds(at, CHUNK), index : index + 1]
        return jnp.broadcast_to(column, (CHUNK, cols)).astype(jnp.bfloat16)

    def own_rows(layer, slot):
        @pl.loop(0, channels // CHUNK)
        def _(block):
            at = pl.multiple_of(block * CHUNK, CHUNK)
            weights = [tap(layer, at, d) for d in range(2 * REACH + 1)]
            totals = [None] * rows
            for source in range(rows):
                x = field[slot, REACH + source, pl.ds(at, CHUNK)]
                for row in range(max(0, source - REACH), min(rows, source + REACH + 1)):
                    term = weights[source - row + REACH] * x
                    totals[row] = term if totals[row] is None else totals[row] + term
            for row in range(rows):
                conv[row, pl.ds(at, CHUNK)] = totals[row].astype(jnp.float32)

    def edge_rows(layer, slot):
        sums[...] = jnp.zeros(sums.shape, jnp.float32)
        lane = lax.broadcasted_iota(jnp.int32, (CHUNK, cols), 1)

        @pl.loop(0, channels // CHUNK)
        def _(block):
            at = pl.multiple_of(block * CHUNK, CHUNK)
            weights = [tap(layer, at, d) for d in range(4 * REACH + 1)]
            near = [field[slot, k, pl.ds(at, CHUNK)] for k in range(rows + 2 * REACH)]
            far = [edge[row, pl.ds(at, CHUNK)] for row in range(rows)]
            held = [conv[row, pl.ds(at, CHUNK)] for row in range(rows)]
            totals = [jnp.zeros((CHUNK, cols), jnp.bfloat16)] * rows
            for row in range(rows):
                for source in range(row - REACH, row + REACH + 1):
                    if source < 0 or source >= rows:
                        x = near[REACH + source]
                        totals[row] = totals[row] + weights[source - row + REACH] * x
            index = 2 * REACH + 1
            for d in range(-REACH, REACH + 1):
                if d == 0:
                    continue
                outside = lane >= cols + d if d < 0 else lane < d
                for row in range(rows):
                    source = jnp.where(outside, far[row], near[REACH + row])
                    totals[row] = totals[row] + weights[index] * pltpu.roll(source, (-d) % cols, 1)
                index += 1
            for row in range(rows):
                total = held[row] + totals[row].astype(jnp.float32)
                square = total * total
                conv[row, pl.ds(at, CHUNK)] = total
                sums[0, row] += total[0:8] + total[8:16]
                sums[1, row] += square[0:8] + square[8:16]

    def mix_pair(layer, slot, following, pair):
        for place, row in enumerate(pair):
            center = jnp.sum(sums[0, row], axis=0, keepdims=True) / channels
            second = jnp.sum(sums[1, row], axis=0, keepdims=True) / channels
            scale = lax.rsqrt(jnp.maximum(second - center * center, 0.0) + epsilon)
            gain = taps[layer, :, 4 * REACH + 1 : 4 * REACH + 2]
            normed[:, place * cols : (place + 1) * cols] = (
                (conv[row] - center) * scale * gain
            ).astype(jnp.bfloat16)

        mixed = jnp.dot(mix[layer], normed[...], preferred_element_type=jnp.float32)
        bent = mixed * (0.7978845608028654 + 0.035677408136300125 * (mixed * mixed))
        half_mixed = 0.5 * mixed
        bump = half_mixed + half_mixed * jnp.tanh(bent)
        held = [field[slot, REACH + row].astype(jnp.float32) for row in pair]
        for place, row in enumerate(pair):
            field[following, REACH + row] = (
                held[place] + bump[:, place * cols : (place + 1) * cols]
            ).astype(jnp.bfloat16)

    encode(0, 0)
    start_lat(0)
    start_lon(0)

    outer = list(range(REACH)) + list(range(rows - 1, rows - 1 - REACH, -1))
    inner = list(range(REACH, rows - REACH))

    def pairs(items):
        return [items[k : k + 2] for k in range(0, len(items), 2)]

    @pl.loop(0, total_layers)
    def _(index):
        slot = index % 2
        following = 1 - slot
        layer = index % layers
        step = index // layers
        last = layer == layers - 1
        own_rows(layer, slot)
        finish(slot)
        edge_rows(layer, slot)
        for pair in pairs(outer):
            mix_pair(layer, slot, following, pair)

        @pl.when(jnp.logical_not(last))
        def _():
            start_lat(following)

        for pair in pairs(inner):
            mix_pair(layer, slot, following, pair)

        @pl.when(last)
        def _():
            for row in range(rows):
                decoded = jnp.dot(
                    decode[...], field[following, REACH + row], preferred_element_type=jnp.float32
                )
                fresh = (current[row].astype(jnp.float32) + decoded).astype(jnp.bfloat16)
                current[row] = fresh
                trajectory[step, row] = fresh

            @pl.when(step < steps - 1)
            def _():
                encode(step + 1, following)
                start_lat(following)

        @pl.when(index < total_layers - 1)
        def _():
            start_lon(following)


def rollout(count, state, noise, encoder_state_weight, enc_noise, lat_taps, lon_taps, gains, mix, decode):
    quantities, rows, cols = state.shape
    steps = noise.shape[1]
    layers, channels, _ = mix.shape
    take, give = edge_maps(rows, cols)
    table = jnp.concatenate([lat_taps, lon_taps, gains[:, None]], axis=1).transpose(0, 2, 1)
    vmem = pl.BlockSpec(memory_space=pltpu.VMEM)
    return pl.pallas_call(
        functools.partial(rollout_kernel, count, layers),
        out_shape=jax.ShapeDtypeStruct((steps, rows, quantities, cols), jnp.bfloat16),
        in_specs=[vmem] * 9,
        out_specs=vmem,
        scratch_shapes=[
            pltpu.VMEM((2, rows + 2 * REACH, channels, cols), jnp.bfloat16),
            pltpu.VMEM((rows, channels, cols), jnp.float32),
            pltpu.VMEM((rows, channels, cols), jnp.bfloat16),
            pltpu.VMEM((rows, quantities, cols), jnp.bfloat16),
            pltpu.VMEM((channels, 2 * cols), jnp.bfloat16),
            pltpu.VMEM((2, rows, 8, cols), jnp.float32),
            pltpu.VMEM((2, channels // 2, cols), jnp.bfloat16),
            pltpu.VMEM((2, channels // 2, cols), jnp.bfloat16),
            pltpu.SemaphoreType.DMA((2, 3)),
            pltpu.SemaphoreType.DMA((2, 3)),
        ],
        compiler_params=pltpu.CompilerParams(
            collective_id=0, has_side_effects=True, vmem_limit_bytes=40 * 1024 * 1024
        ),
    )(
        state.transpose(1, 0, 2),
        noise[0].transpose(0, 2, 1, 3),
        table,
        encoder_state_weight,
        enc_noise,
        mix,
        decode,
        jnp.asarray(take, jnp.bfloat16),
        jnp.asarray(give, jnp.bfloat16),
    )


def local(
    count, state, noise, target, encoder_state_weight, enc_noise, lat_taps, lon_taps, gains, mix, decode
):
    quantity_total = state.shape[0]
    forecast = rollout(
        count, state, noise, encoder_state_weight, enc_noise, lat_taps, lon_taps, gains, mix, decode
    )
    trajectory_predictions = forecast.transpose(0, 2, 1, 3)[None]
    members = lax.axis_size("member")
    scale = float(members)
    regrouped = lax.all_to_all(
        trajectory_predictions, "member", split_axis=2, concat_axis=0, tiled=True
    )
    quantities_real = regrouped.astype(jnp.float32)
    block = quantity_total // members
    start = lax.axis_index("member") * block
    target_block = lax.dynamic_slice_in_dim(target, start, block, 1).astype(jnp.float32)
    skill = jnp.sum(jnp.abs(quantities_real - target_block[None]), axis=(0, 1))
    spread = jnp.zeros(skill.shape, jnp.float32)
    for other in range(members):
        spread = spread + jnp.sum(jnp.abs(quantities_real - quantities_real[other][None]), axis=(0, 1))
    probabilistic_error = skill / scale - spread / (2.0 * scale * (scale - 1.0))
    return (trajectory_predictions, probabilistic_error)


def solution(mesh):
    assert mesh.shape["lon"] == 2
    in_specs = (
        P(None, "lat", "lon"),
        P("member", None, None, "lat", "lon"),
        P(None, None, "lat", "lon"),
        P(),
        P(),
        P(),
        P(),
        P(),
        P(),
        P(),
    )
    out_specs = (P("member", None, None, "lat", "lon"), P("member", "lat", "lon"))
    return jax.shard_map(
        functools.partial(local, mesh.shape["lat"]),
        mesh=mesh,
        in_specs=in_specs,
        out_specs=out_specs,
        check_vma=False,
    )
```
